32 devices in a mesh: az: 8 (over y, x, core), el: 4 (over z).
Axes of the slice: x: 2, y: 2, z: 4, core: 2. Of those that a mesh axis runs over, the one named last changes fastest.
Arguments:
- features: bfloat16 [64, 128, 2048], P(None, 'el', 'az'), may hold values from -30 to 30
- points_xyz: bfloat16 [3, 128, 2048], P(None, 'el', 'az'), may hold values from -4 to 4
- return_mask: int32 [128, 2048], P('el', 'az'), may hold values 0 or 1
- owner_tile: int32 [128, 2048], P('el', 'az'), may hold values from 0 to 31, as said below
- bev_cell: int32 [128, 2048], P('el', 'az'), may hold values from 0 to 2047
- meta_proj: float32 [2, 3, 64], replicated, may hold values from -3.5 to 3.5
- meta_bias: float32 [2, 64], replicated, may hold values from -4 to 4
- conv_weight: bfloat16 [2, 9, 64, 64], replicated, may hold values from -0.25 to 0.25
- norm_gain: float32 [2, 64], replicated, may hold values from 0.25 to 1.75
- head_weight: bfloat16 [9, 64, 128], replicated, may hold values from -0.25 to 0.25
- head_bias: float32 [128], replicated, may hold values from -3 to 3
Outputs:
- head_features: bfloat16 [128, 128, 512], P(None, 'az', 'el')
The draws below stay inside these ranges and needn't reach their ends.
Inputs may be any that keep to these rules, and one draw needn't show every extreme that they name: `owner_tile`: among the pixels of one elevation band of 32 rows and one azimuth sector of 256 columns, at most 512 name the same tile; in every draw some tile is named exactly 512 times by every such block.
All inputs are finite; a program needn't handle non-finite values. No bound on the sum of `return_mask` on one device may be relied on, other than what follows from the above.
Results may differ from the reference program's by a relative error of at most 0.0054.
Values may be sent and summed in bfloat16 or wider, within the bound.
A program may use at most 64 MiB of HBM per device.

```python
import math
import jax
import jax.numpy as jnp
from jax import lax

CH = 64
HEAD_CH = 128
LAYERS = 2
ROWS_DEV = 32
COLS_DEV = 256
TILE_Y = 16
TILE_X = 128
TILE = 2048
ROWS = 128
COLS = 2048
BEV_Y = 128
BEV_X = 512
CAP = 512
N_AZ = 8
N_EL = 4


def draw_features(key, part):
    key = jax.random.fold_in(key, 5)
    keys = jax.random.split(key, 3)
    channel = jnp.exp(jax.random.uniform(keys[0], (CH, 1, 1), jnp.float32, math.log(0.3), math.log(3.0)))
    pixel = jnp.exp(jax.random.uniform(keys[1], (1, ROWS, COLS), jnp.float32, -0.7, 0.7))
    base = jax.random.truncated_normal(keys[2], -3.0, 3.0, (CH, ROWS, COLS), jnp.float32)
    return (base * channel * pixel).astype(jnp.bfloat16)


def draw_owner_tile(key, part):
    key = jax.random.fold_in(key, 11)
    keys = jax.random.split(key, 4)
    n_el = ROWS // ROWS_DEV
    n_az = COLS // COLS_DEV
    devices = n_el * n_az
    count_pts = ROWS_DEV * COLS_DEV
    slots_all = devices * CAP
    tiers = jax.random.randint(keys[0], (devices,), 0, 4)
    hottest = jax.random.randint(keys[1], (), 0, devices)
    scores = jax.random.randint(keys[2], (devices, devices, CAP), 0, 4096) + tiers[None, :, None] * 1024 + 1
    scores = jnp.where(jnp.arange(devices)[None, :, None] == hottest, 0, scores)
    ranked = scores.reshape(devices, slots_all) * slots_all + jnp.arange(slots_all, dtype=jnp.int32)[None, :]
    chosen = jnp.argsort(ranked, axis=1)[:, :count_pts]
    owners = (chosen // CAP).astype(jnp.int32)
    shuffle_keys = jax.random.split(keys[3], devices)
    owners = jax.vmap(lambda sub, row: jax.random.permutation(sub, row))(shuffle_keys, owners)
    owners = owners.reshape(n_az, n_el, ROWS_DEV, COLS_DEV).transpose(1, 2, 0, 3)
    return owners.reshape(ROWS, COLS).astype(jnp.int32)


def place_ends(entries, key, least, high):
    extent = entries.shape
    place = [jax.random.randint(jax.random.fold_in(key, axis), (), 0, extent[axis]) for axis in range(len(extent))]
    entries = entries.at[tuple(place)].set(least)
    longest = extent.index(max(extent))
    place[longest] = (place[longest] + 1) % extent[longest]
    return entries.at[tuple(place)].set(high)


def steps_of(stream_key, dims, cuts, least, top_value):
    gain, own = 1.0, jax.random.fold_in(stream_key, 6)
    for axis_at, blocks in cuts:
        draws = jnp.exp(jax.random.uniform(jax.random.fold_in(own, axis_at), (blocks,), jnp.float32, least / len(cuts), top_value / len(cuts)))
        gain = gain * jnp.repeat(draws, dims[axis_at] // blocks).reshape([-1 if axis == axis_at else 1 for axis in range(len(dims))])
    return gain


def noise(stream_key, shape, spread, limit, pieces=(), kind=jnp.bfloat16):
    gain = steps_of(stream_key, shape, pieces, -0.22, 0.18) if pieces else 1.0
    drawn = jax.random.normal(stream_key, shape, jnp.float32) * spread * gain
    return jnp.minimum(jnp.maximum(drawn, -limit), limit).astype(kind)


def setup_inputs(seed: int = 0) -> dict:
    splits = jax.random.split(jax.random.key(seed), 12)
    features = draw_features(jax.random.fold_in(splits[11], 71), 0)
    points_xyz = noise(splits[1], (3, ROWS, COLS), 1.0, 4.0, ((1, 4), (2, 8)))
    return_mask = place_ends((jax.random.randint(splits[2], (ROWS, COLS), 0, 10) < 9).astype(jnp.int32), jax.random.fold_in(splits[2], 1), 0, 1)
    owner_tile = draw_owner_tile(jax.random.fold_in(splits[11], 71), 0)
    bev_cell = place_ends(jax.random.randint(splits[4], (ROWS, COLS), 0, TILE), jax.random.fold_in(splits[4], 1), 0, TILE - 1).astype(jnp.int32)
    meta_proj = noise(splits[5], (LAYERS, 3, CH), 3 ** -0.5, 3.5, (), jnp.float32)
    meta_bias = noise(splits[6], (LAYERS, CH), 1.0, 4.0, (), jnp.float32)
    conv_weight = noise(splits[7], (LAYERS, 9, CH, CH), (9 * CH) ** -0.5, 0.25)
    norm_gain = jnp.clip(1.0 + 0.15 * jax.random.normal(splits[8], (LAYERS, CH), jnp.float32), 0.25, 1.75)
    head_weight = noise(splits[9], (9, CH, HEAD_CH), (9 * CH) ** -0.5, 0.25)
    head_bias = noise(splits[10], (HEAD_CH,), 0.5, 3.0, (), jnp.float32)
    return dict(features=features, points_xyz=points_xyz, return_mask=return_mask, owner_tile=owner_tile, bev_cell=bev_cell, meta_proj=meta_proj, meta_bias=meta_bias, conv_weight=conv_weight, norm_gain=norm_gain, head_weight=head_weight, head_bias=head_bias)


def meta_layer(padded, places, validity, project, offsets, kernel, scales):
    height = padded.shape[1] - 2
    breadth = padded.shape[2] - 2
    middle = places[:, 1:1 + height, 1:1 + breadth].astype(jnp.float32)
    summed = jnp.zeros((kernel.shape[2], height, breadth), jnp.float32)
    for k in range(9):
        a = k // 3
        b = k % 3
        beside = padded[:, a:a + height, b:b + breadth]
        relative = places[:, a:a + height, b:b + breadth].astype(jnp.float32) - middle
        logits = offsets[:, None, None] + relative[0][None] * project[0][:, None, None]
        logits = logits + relative[1][None] * project[1][:, None, None]
        logits = logits + relative[2][None] * project[2][:, None, None]
        gating = jax.nn.sigmoid(logits)
        weighted = (gating * beside.astype(jnp.float32)).astype(jnp.bfloat16)
        summed = summed + jnp.einsum('cd,chw->dhw', kernel[k].astype(jnp.float32), weighted.astype(jnp.float32), precision=lax.Precision.HIGHEST)
    scaled = summed * lax.rsqrt(lax.optimization_barrier(jnp.mean(summed * summed, axis=0)) + 1e-06) * scales[:, None, None]
    middle_feat = padded[:, 1:1 + height, 1:1 + breadth].astype(jnp.float32)
    return ((middle_feat + jnp.maximum(scaled, 0.0)) * validity).astype(jnp.bfloat16)

def wrap_pad(image):
    image = jnp.concatenate([image[:, :, -1:], image, image[:, :, :1]], axis=2)
    return jnp.pad(image, ((0, 0), (1, 1), (0, 0)))

def whole_layer(image, points_xyz, mask_float, project, offsets, kernel, scales):
    padded = wrap_pad(image)
    places = wrap_pad(points_xyz)

    def sector(index):
        start = (index * COLS_DEV).astype(jnp.int32)
        piece = lax.dynamic_slice_in_dim(padded, start, COLS_DEV + 2, 2)
        spots = lax.dynamic_slice_in_dim(places, start, COLS_DEV + 2, 2)
        valid_piece = lax.dynamic_slice_in_dim(mask_float, start, COLS_DEV, 1)
        return meta_layer(piece, spots, valid_piece, project, offsets, kernel, scales)
    blocks = lax.map(sector, jnp.arange(N_AZ, dtype=jnp.int32))
    return blocks.transpose(1, 2, 0, 3).reshape(CH, ROWS, COLS)

def reference(features, points_xyz, return_mask, owner_tile, bev_cell, meta_proj, meta_bias, conv_weight, norm_gain, head_weight, head_bias):
    mask_float = return_mask.astype(jnp.float32)
    image = features * return_mask.astype(jnp.bfloat16)
    for layer in range(LAYERS):
        image = whole_layer(image, points_xyz, mask_float, meta_proj[layer], meta_bias[layer], conv_weight[layer], norm_gain[layer])
    points = image.reshape(CH, ROWS * COLS).T.astype(jnp.float32)
    owners = owner_tile.reshape(-1)
    cells = bev_cell.reshape(-1)
    keep = mask_float.reshape(-1)
    tile_row = owners // N_EL
    tile_col = owners % N_EL
    target = (tile_row * TILE_Y + cells // TILE_X) * BEV_X + tile_col * TILE_X + cells % TILE_X
    sums = jax.ops.segment_sum(points * keep[:, None], target, BEV_Y * BEV_X)
    counts = jax.ops.segment_sum(keep, target, BEV_Y * BEV_X)
    grid = (sums / jnp.maximum(counts, 1.0)[:, None]).astype(jnp.bfloat16)
    grid = grid.reshape(BEV_Y, BEV_X, CH).transpose(2, 0, 1)
    framed = jnp.pad(grid, ((0, 0), (1, 1), (1, 1)))
    summed = jnp.zeros((HEAD_CH, BEV_Y, BEV_X), jnp.float32)
    for k in range(9):
        a = k // 3
        b = k % 3
        patch = framed[:, a:a + BEV_Y, b:b + BEV_X]
        summed = summed + jnp.einsum('cd,chw->dhw', head_weight[k].astype(jnp.float32), patch.astype(jnp.float32), precision=lax.Precision.HIGHEST)
    return jnp.maximum(summed + head_bias[:, None, None], 0.0).astype(jnp.bfloat16)
```

```python
import jax
import jax.numpy as jnp
from jax import lax
from jax.experimental import pallas as pl
from jax.experimental.pallas import tpu as pltpu
from jax.sharding import PartitionSpec as P

CH = 64
HEAD_CH = 128
TILE_Y = 16
TILE_X = 128
F32 = jnp.float32
BF16 = jnp.bfloat16
WIDE = 144


def padded_2(cells, sides, width, closed):
    for axis, dim in sides:
        count = lax.axis_size(axis)
        ends = count if closed else count - 1
        head = lax.slice_in_dim(cells, 0, width, axis=dim)
        tail = lax.slice_in_dim(cells, cells.shape[dim] - width, cells.shape[dim], axis=dim)
        cells = jnp.concatenate(
            [
                lax.ppermute(tail, axis, [(i, (i + 1) % count) for i in range(ends)]),
                cells,
                lax.ppermute(head, axis, [((i + 1) % count, i) for i in range(ends)]),
            ],
            axis=dim,
        )
    return cells


def slot_ranks(owners, devices):
    count_pts = owners.shape[0]
    group = min(128, count_pts)
    member = (owners[:, None] == jnp.arange(devices, dtype=jnp.int32)[None, :]).astype(BF16)
    blocks = member.reshape(count_pts // group, group, devices)
    lower = (
        lax.broadcasted_iota(jnp.int32, (group, group), 0)
        > lax.broadcasted_iota(jnp.int32, (group, group), 1)
    ).astype(BF16)
    inside = jnp.einsum("ij,bjd->bid", lower, blocks, preferred_element_type=F32)
    totals = jnp.sum(blocks, axis=1, dtype=F32)
    before = jnp.cumsum(totals, axis=0) - totals
    ranks = jnp.sum(jnp.where(blocks > 0, inside + before[:, None, :], 0.0), axis=2)
    return ranks.reshape(-1).astype(jnp.int32)


def layers_kernel(
    height, tiles, cap,
    tgt_ref, xp_ref, aux_ref, waux_ref, bias_ref, gain_ref, conv_ref, mean_ref, lab_ref,
    msg_ref,
    q1, q2, mk, x0, x1, wt, pts, dest,
):
    @pl.loop(0, height + 4)
    def _(r):
        got = jnp.dot(aux_ref[r], waux_ref[...], preferred_element_type=F32)
        q1[r] = got[:, 0:128]
        q2[r] = got[:, 128:256]
        mk[r] = got[:, 256:384]
        x0[r] = xp_ref[r].astype(F32) * (got[:, 256:384] * 0.5)

    def layer(l, rows, width, per, q, x, qrow, qcol, emit):
        @pl.loop(0, rows // per)
        def _(s):
            for u in range(per):
                r = s * per + u
                shift = q[r + 1 + qrow, pl.ds(1 + qcol, width), :] - bias_ref[l : l + 1, :]
                for k in range(9):
                    a, b = k // 3, k % 3
                    arg = q[r + a + qrow, pl.ds(b + qcol, width), :] - shift
                    half = x[r + a, pl.ds(b, width), :]
                    wt[pl.ds(u * width, width), k * 128 : (k + 1) * 128] = (
                        half + half * jnp.tanh(arg)
                    ).astype(BF16)
            y = jnp.dot(wt[0 : per * width, :], conv_ref[l], preferred_element_type=F32)
            ms = jnp.dot((y * y).astype(BF16), mean_ref[...], preferred_element_type=F32)
            act = jnp.maximum(y * lax.rsqrt(ms + 1e-6) * gain_ref[l : l + 1, :], 0.0)
            for u in range(per):
                r = s * per + u
                new = x[r + 1, pl.ds(1, width), :] * 2.0 + act[u * width : (u + 1) * width, :]
                new = new * mk[r + 1 + qrow, pl.ds(1 + qcol, width), :]
                emit(r, new.astype(BF16).astype(F32))

    def emit1(r, new):
        x1[r] = new * 0.5

    def emit2(r, new):
        pts[pl.ds(pl.multiple_of(r * 256, 256), 128), :] = new
        pts[pl.ds(pl.multiple_of(r * 256 + 128, 128), 128), :] = pltpu.roll(new, 64, 1)

    layer(0, height + 2, 136, 2, q1, x0, 0, 0, emit1)
    layer(1, height, 128, 4, q2, x1, 1, 1, emit2)

    unroll = 64

    @pl.loop(0, height * 256 // unroll)
    def _(i):
        base = i * unroll
        for u in range(unroll):
            dest[pl.ds(tgt_ref[base + u], 1), :] = pts[pl.ds(base + u, 1), :]

    left = lax.broadcasted_iota(jnp.int32, (cap // 2, 128), 1) < 64

    @pl.loop(0, tiles)
    def _(t):
        low = dest[pl.ds(pl.multiple_of(t * cap, cap), cap // 2), :]
        high = dest[pl.ds(pl.multiple_of(t * cap + cap // 2, cap // 2), cap // 2), :]
        msg_ref[t, 0 : cap // 2, :] = jnp.where(left, low, pltpu.roll(high, 64, 1)).astype(BF16)
        msg_ref[t, cap // 2 : cap // 2 + 16, :] = lab_ref[t]


def cells_kernel(cap, per, msg_ref, out_ref, acc):
    s = pl.program_id(0)

    @pl.when(s == 0)
    def _():
        acc[...] = jnp.zeros_like(acc)

    half = cap // 2
    size = per * cap
    codes = lax.broadcasted_iota(jnp.int32, (256, 1), 0).astype(F32).astype(BF16)
    his, los, feats = [], [], []
    for p in range(per):
        body = jnp.transpose(msg_ref[p, 0:half, :])
        labels = msg_ref[p, half : half + 16, :]
        lanes = min(cap, 128)
        for j in range(cap // lanes):
            his.append(labels[j : j + 1, 0:lanes])
            los.append(labels[8 + j : 9 + j, 0:lanes])
        feats.append(body[0:64, :])
        feats.append(body[64:128, :])
    hi = jnp.concatenate(his, axis=1)
    lo = jnp.concatenate(los, axis=1)
    feat = jnp.concatenate(feats, axis=1)
    zero = jnp.zeros((64, size), BF16)
    parts = [jnp.where(hi == jnp.array(k, BF16), feat, zero) for k in range(8)]
    marks = lax.broadcasted_iota(jnp.int32, (16, 1), 0).astype(F32).astype(BF16)
    one = jnp.ones((16, size), BF16)
    parts.append(jnp.where(marks == hi, one, jnp.zeros((16, size), BF16)))
    lhs = jnp.concatenate(parts, axis=0)
    rhs = jnp.where(codes == lo, jnp.ones((256, size), BF16), jnp.zeros((256, size), BF16))
    acc[...] += lax.dot_general(
        lhs, rhs, (((1,), (1,)), ((), ())), preferred_element_type=F32
    )

    @pl.when(s == pl.num_programs(0) - 1)
    def _():
        for h in range(8):
            inv = jnp.maximum(acc[512 + h : 513 + h, :], 1.0)
            bev = (acc[h * 64 : (h + 1) * 64, :] / inv).astype(BF16)
            out_ref[2 * h] = bev[:, 0:128]
            out_ref[2 * h + 1] = bev[:, 128:256]


def block_pair(w):
    zero = jnp.zeros_like(w)
    return jnp.concatenate(
        [jnp.concatenate([w, zero], axis=-1), jnp.concatenate([zero, w], axis=-1)], axis=-2
    )


def on_device(
    features, points_xyz, return_mask, owner_tile, bev_cell,
    meta_proj, meta_bias, conv_weight, norm_gain, head_weight, head_bias,
):
    height, breadth = return_mask.shape
    az_count = lax.axis_size("az")
    el_count = lax.axis_size("el")
    devices = az_count * el_count
    count_pts = height * breadth
    cap = 2 * count_pts // devices

    stacked = jnp.concatenate([features, points_xyz, return_mask.astype(BF16)[None]], axis=0)
    stacked = padded_2(stacked, (("az", 2),), 2, True)
    stacked = padded_2(stacked, (("el", 1),), 2, False)
    turned = stacked.transpose(1, 2, 0)
    first, last = turned[:, 0:132], turned[:, 128:260]
    grow = ((0, 0), (0, WIDE - 132), (0, 0))
    xp = jnp.pad(jnp.concatenate([first[..., :CH], last[..., :CH]], axis=2), grow)
    spots = jnp.concatenate([first[..., CH:], last[..., CH:]], axis=2)
    aux = jnp.pad(
        jnp.concatenate([spots, spots, spots], axis=2), ((0, 0), (0, WIDE - 132), (0, 8))
    )

    proj = meta_proj * 0.5
    top = lax.reduce_precision(proj, 8, 7)
    mid = lax.reduce_precision(proj - top, 8, 7)
    low = lax.reduce_precision(proj - top - mid, 8, 7)
    rows = []
    for i, part in enumerate((top, mid, low)):
        flag = jnp.full((1, CH), 1.0 if i == 0 else 0.0, F32)
        nil3, nil1 = jnp.zeros((3, CH), F32), jnp.zeros((1, CH), F32)
        wide = [
            block_pair(jnp.concatenate([part[0], nil1], axis=0)),
            block_pair(jnp.concatenate([part[1], nil1], axis=0)),
            block_pair(jnp.concatenate([nil3, flag], axis=0)),
        ]
        rows.append(jnp.concatenate(wide, axis=1))
    waux = jnp.pad(jnp.concatenate(rows, axis=0), ((0, 8), (0, 0))).astype(BF16)
    bias = jnp.concatenate([meta_bias, meta_bias], axis=1) * 0.5
    gain = jnp.concatenate([norm_gain, norm_gain], axis=1)
    conv = block_pair(conv_weight).reshape(2, 9 * 128, 128)
    mean = block_pair(jnp.full((CH, CH), 1.0 / CH, BF16))

    owners = owner_tile.reshape(-1)
    cells = bev_cell.reshape(-1)
    keep = return_mask.reshape(-1)
    ranks = slot_ranks(owners, devices)
    target = owners * cap + ranks
    member = owners[None, :] == jnp.arange(devices, dtype=jnp.int32)[:, None]
    hi = jnp.where(keep > 0, cells // 256 + 1, 0)
    lo = jnp.where(keep > 0, cells % 256 + 1, 0)
    value = jnp.stack([hi, lo], axis=0).astype(BF16)
    left = jnp.where(member[None], value[:, None, :], 0).astype(BF16)
    right = (ranks[:, None] == jnp.arange(cap, dtype=jnp.int32)[None, :]).astype(BF16)
    labels = jnp.einsum("vtp,pr->tvr", left, right, preferred_element_type=F32) - 1.0
    lanes = min(cap, 128)
    labels = labels.reshape(devices, 2, cap // lanes, lanes)
    labels = jnp.pad(
        labels, ((0, 0), (0, 0), (0, 8 - cap // lanes), (0, 128 - lanes))
    ).reshape(devices, 16, 128).astype(BF16)

    vm = pl.BlockSpec(memory_space=pltpu.VMEM)
    deep = cap // 2 + 16
    plane = pltpu.VMEM((height + 4, WIDE, 128), F32)
    msg = pl.pallas_call(
        lambda *refs: layers_kernel(height, devices, cap, *refs),
        out_shape=jax.ShapeDtypeStruct((devices, deep, 128), BF16),
        in_specs=[pl.BlockSpec(memory_space=pltpu.SMEM)] + [vm] * 8,
        out_specs=vm,
        scratch_shapes=[
            plane, plane, plane, plane,
            pltpu.VMEM((height + 2, 136, 128), F32),
            pltpu.VMEM((512, 9 * 128), BF16),
            pltpu.VMEM((count_pts, 128), F32),
            pltpu.VMEM((devices * cap, 128), F32),
        ],
        compiler_params=pltpu.CompilerParams(vmem_limit_bytes=56 << 20),
        name="layers",
    )(target, xp, aux, waux, bias, gain, conv, mean, labels)

    got = lax.all_to_all(msg, ("az", "el"), split_axis=0, concat_axis=0, tiled=True)

    per = max(1, 512 // cap)
    grid = pl.pallas_call(
        lambda *refs: cells_kernel(cap, per, *refs),
        out_shape=jax.ShapeDtypeStruct((TILE_Y, CH, TILE_X), BF16),
        grid=(devices // per,),
        in_specs=[pl.BlockSpec((per, deep, 128), lambda s: (s, 0, 0))],
        out_specs=pl.BlockSpec((TILE_Y, CH, TILE_X), lambda s: (0, 0, 0)),
        scratch_shapes=[pltpu.VMEM((528, 256), F32)],
        compiler_params=pltpu.CompilerParams(vmem_limit_bytes=56 << 20),
        name="cells",
    )(got)

    framed = padded_2(grid, (("az", 0), ("el", 2)), 1, False)
    summed = jnp.zeros((HEAD_CH, TILE_Y, TILE_X), F32)
    for k in range(9):
        a = k // 3
        b = k % 3
        summed = summed + jnp.einsum(
            "cd,hcw->dhw",
            head_weight[k],
            framed[a : a + TILE_Y, :, b : b + TILE_X],
            preferred_element_type=F32,
        )
    return jnp.maximum(summed + head_bias[:, None, None], 0.0).astype(BF16)


def solution(mesh):
    placed = (
        P(None, "el", "az"),
        P(None, "el", "az"),
        P("el", "az"),
        P("el", "az"),
        P("el", "az"),
        P(),
        P(),
        P(),
        P(),
        P(),
        P(),
    )
    return jax.shard_map(
        on_device, mesh=mesh, in_specs=placed, out_specs=P(None, "az", "el"), check_vma=False
    )
```

```python
import jax
import jax.numpy as jnp
from jax import lax
from jax.experimental import pallas as pl
from jax.experimental.pallas import tpu as pltpu
from jax.sharding import PartitionSpec as P

CH = 64
HEAD_CH = 128
TILE_Y = 16
TILE_X = 128
F32 = jnp.float32
BF16 = jnp.bfloat16
WIDE = 144


def slot_ranks(owners, devices):
    count_pts = owners.shape[0]
    group = min(128, count_pts)
    member = (owners[:, None] == jnp.arange(devices, dtype=jnp.int32)[None, :]).astype(BF16)
    blocks = member.reshape(count_pts // group, group, devices)
    lower = (
        lax.broadcasted_iota(jnp.int32, (group, group), 0)
        > lax.broadcasted_iota(jnp.int32, (group, group), 1)
    ).astype(BF16)
    inside = jnp.einsum("ij,bjd->bid", lower, blocks, preferred_element_type=F32)
    totals = jnp.sum(blocks, axis=1, dtype=F32)
    before = jnp.cumsum(totals, axis=0) - totals
    ranks = jnp.sum(jnp.where(blocks > 0, inside + before[:, None, :], 0.0), axis=2)
    return ranks.reshape(-1).astype(jnp.int32)


def layers_kernel(
    height, tiles, cap,
    tgt_ref, main_ref, left_ref, right_ref, top_ref, low_ref,
    waux_ref, bias_ref, gain_ref, conv_ref, mean_ref, lab_ref,
    msg_ref,
    q1, q2, mk, x0, x1, wt, pts, dest, line,
):
    line[...] = jnp.zeros_like(line)

    def place(slot, r):
        pair = jnp.concatenate(
            [line[slot, 0:WIDE, :].astype(BF16), line[slot, 128 : 128 + WIDE, :].astype(BF16)],
            axis=1,
        )
        got = jnp.dot(pair, waux_ref[...], preferred_element_type=F32)
        q1[r] = got[:, 0:128]
        q2[r] = got[:, 128:256]
        mk[r] = got[:, 256:384]
        x0[r] = got[:, 384:512] * (got[:, 256:384] * 0.5)

    for r in range(2):
        line[r, 0:260, :] = top_ref[r].astype(F32)
        place(r, r)
    for r in range(2):
        line[r, 0:260, :] = low_ref[r].astype(F32)
        place(r, height + 2 + r)

    @pl.loop(0, height // 2)
    def _(s):
        for u in range(2):
            r = s * 2 + u
            line[u, 0:2, :] = left_ref[r].astype(F32)
            line[u, 2:258, :] = main_ref[r].astype(F32)
            line[u, 258:260, :] = right_ref[r].astype(F32)
            place(u, r + 2)

    def layer(l, rows, width, per, q, x, qrow, qcol, emit):
        @pl.loop(0, rows // per)
        def _(s):
            for u in range(per):
                r = s * per + u
                shift = q[r + 1 + qrow, pl.ds(1 + qcol, width), :] - bias_ref[l : l + 1, :]
                for k in range(9):
                    a, b = k // 3, k % 3
                    arg = q[r + a + qrow, pl.ds(b + qcol, width), :] - shift
                    half = x[r + a, pl.ds(b, width), :]
                    wt[pl.ds(u * width, width), k * 128 : (k + 1) * 128] = (
                        half + half * jnp.tanh(arg)
                    ).astype(BF16)
            y = jnp.dot(wt[0 : per * width, :], conv_ref[l], preferred_element_type=F32)
            ms = jnp.dot((y * y).astype(BF16), mean_ref[...], preferred_element_type=F32)
            act = jnp.maximum(y * lax.rsqrt(ms + 1e-6) * gain_ref[l : l + 1, :], 0.0)
            for u in range(per):
                r = s * per + u
                new = x[r + 1, pl.ds(1, width), :] * 2.0 + act[u * width : (u + 1) * width, :]
                new = new * mk[r + 1 + qrow, pl.ds(1 + qcol, width), :]
                emit(r, new.astype(BF16).astype(F32))

    def emit1(r, new):
        x1[r] = new * 0.5

    def emit2(r, new):
        pts[pl.ds(pl.multiple_of(r * 256, 256), 128), :] = new
        pts[pl.ds(pl.multiple_of(r * 256 + 128, 128), 128), :] = pltpu.roll(new, 64, 1)

    layer(0, height + 2, 136, 2, q1, x0, 0, 0, emit1)
    layer(1, height, 128, 4, q2, x1, 1, 1, emit2)

    unroll = 64

    @pl.loop(0, height * 256 // unroll)
    def _(i):
        base = i * unroll
        for u in range(unroll):
            dest[pl.ds(tgt_ref[base + u], 1), :] = pts[pl.ds(base + u, 1), :]

    left = lax.broadcasted_iota(jnp.int32, (cap // 2, 128), 1) < 64

    @pl.loop(0, tiles)
    def _(t):
        low = dest[pl.ds(pl.multiple_of(t * cap, cap), cap // 2), :]
        high = dest[pl.ds(pl.multiple_of(t * cap + cap // 2, cap // 2), cap // 2), :]
        msg_ref[t, 0 : cap // 2, :] = jnp.where(left, low, pltpu.roll(high, 64, 1)).astype(BF16)
        msg_ref[t, cap // 2 : cap // 2 + 16, :] = lab_ref[t]


def cells_kernel(
    cap, az_count, el_count,
    msg_ref, head_ref, bias_ref,
    out_ref,
    got, acc, bev, edges, rims, ends, views,
    send_sem, recv_sem, rim_send, rim_recv,
):
    az, el = lax.axis_index("az"), lax.axis_index("el")
    devices = az_count * el_count
    me = az * el_count + el
    mesh_id = pl.DeviceIdType.MESH

    barrier = pltpu.get_barrier_semaphore()

    def spot(d):
        other = lax.rem(me + d, devices)
        return other, (other // el_count, lax.rem(other, el_count))

    @pl.loop(1, devices)
    def _(d):
        pl.semaphore_signal(barrier, inc=1, device_id=spot(d)[1], device_id_type=mesh_id)

    pl.semaphore_wait(barrier, devices - 1)

    def message(d):
        other, where = spot(d)
        return pltpu.make_async_remote_copy(
            src_ref=msg_ref.at[other],
            dst_ref=got.at[d],
            send_sem=send_sem.at[d],
            recv_sem=recv_sem.at[d],
            device_id=where,
            device_id_type=mesh_id,
        )

    @pl.loop(1, devices)
    def _(d):
        message(d).start()

    half = cap // 2
    lanes = min(cap, 128)
    codes = lax.broadcasted_iota(jnp.int32, (256, 1), 0).astype(F32).astype(BF16)
    marks = lax.broadcasted_iota(jnp.int32, (16, 1), 0).astype(F32).astype(BF16)
    zero = jnp.zeros((64, cap), BF16)

    def add(block, labels):
        body = jnp.transpose(block)
        count = cap // lanes
        hi = jnp.concatenate([labels[j : j + 1, 0:lanes] for j in range(count)], axis=1)
        lo = jnp.concatenate([labels[8 + j : 9 + j, 0:lanes] for j in range(count)], axis=1)
        feat = jnp.concatenate([body[0:64, :], body[64:128, :]], axis=1)
        parts = [jnp.where(hi == jnp.array(k, BF16), feat, zero) for k in range(8)]
        parts.append(
            jnp.where(marks == hi, jnp.ones((16, cap), BF16), jnp.zeros((16, cap), BF16))
        )
        rhs = jnp.where(codes == lo, jnp.ones((256, cap), BF16), jnp.zeros((256, cap), BF16))
        return lax.dot_general(
            jnp.concatenate(parts, axis=0), rhs, (((1,), (1,)), ((), ())),
            preferred_element_type=F32,
        )

    acc[...] = add(msg_ref[me, 0:half, :], msg_ref[me, half : half + 16, :])

    @pl.loop(1, devices)
    def _(d):
        message(d).wait_recv()
        acc[...] += add(got[d, 0:half, :], got[d, half : half + 16, :])

    for h in range(8):
        inv = jnp.maximum(acc[512 + h : 513 + h, :], 1.0)
        mean = (acc[h * 64 : (h + 1) * 64, :] / inv).astype(BF16).astype(F32)
        bev[2 * h + 1] = mean[:, 0:128]
        bev[2 * h + 2] = mean[:, 128:256]

    lane = lax.broadcasted_iota(jnp.int32, (64, 128), 1)
    first = jnp.zeros((64, 128), F32)
    last = jnp.zeros((64, 128), F32)
    for r in range(TILE_Y):
        row = bev[r + 1]
        first = jnp.where(lane == r, row if r == 0 else pltpu.roll(row, r, 1), first)
        last = jnp.where(lane == r, pltpu.roll(row, r + 1, 1), last)
    edges[0] = first.astype(BF16)
    edges[1] = last.astype(BF16)
    edges[2] = bev[1].astype(BF16)
    edges[3] = bev[TILE_Y].astype(BF16)

    plans = []
    for dy in (-1, 0, 1):
        for dx in (-1, 0, 1):
            if dx == 0 and dy == 0:
                continue
            source = (0 if dx < 0 else 1) if dx else (2 if dy < 0 else 3)
            plans.append((dy, dx, source))
    copies = []
    for i, (dy, dx, source) in enumerate(plans):
        copy = pltpu.make_async_remote_copy(
            src_ref=edges.at[source],
            dst_ref=rims.at[i],
            send_sem=rim_send.at[i],
            recv_sem=rim_recv.at[i],
            device_id=(lax.rem(az + dy + az_count, az_count), lax.rem(el + dx + el_count, el_count)),
            device_id_type=mesh_id,
        )
        copy.start()
        copies.append(copy)

    @pl.loop(1, devices)
    def _(d):
        message(d).wait_send()

    for copy in copies:
        copy.wait()

    def rim(y, x):
        i = [(p[0], p[1]) for p in plans].index((-y, -x))
        there = jnp.logical_and(
            jnp.logical_and(az + y >= 0, az + y < az_count),
            jnp.logical_and(el + x >= 0, el + x < el_count),
        )
        return rims[i].astype(F32) * jnp.where(there, 1.0, 0.0)

    bev[0] = rim(-1, 0)
    bev[TILE_Y + 1] = rim(1, 0)
    for j, (y, x) in enumerate([(0, -1), (0, 1), (-1, -1), (-1, 1), (1, -1), (1, 1)]):
        ends[j] = rim(y, x)
    for r in range(TILE_Y + 2):
        row = bev[r]
        if r == 0:
            lhs, rhs, at = ends[2], ends[3], TILE_Y - 1
        elif r == TILE_Y + 1:
            lhs, rhs, at = ends[4], ends[5], 0
        else:
            lhs, rhs, at = ends[0], ends[1], r - 1
        before = lhs if at == 0 else pltpu.roll(lhs, 128 - at, 1)
        after = pltpu.roll(rhs, 127 - at, 1)
        views[r * 192 : r * 192 + 64, :] = jnp.where(
            lane == 0, before, pltpu.roll(row, 1, 1)
        ).astype(BF16)
        views[r * 192 + 64 : r * 192 + 128, :] = row.astype(BF16)
        views[r * 192 + 128 : r * 192 + 192, :] = jnp.where(
            lane == 127, after, pltpu.roll(row, 127, 1)
        ).astype(BF16)

    for s in range(TILE_Y // 2):
        r = 2 * s
        stack = jnp.concatenate(
            [views[r * 192 : r * 192 + 576, :], views[(r + 1) * 192 : (r + 1) * 192 + 576, :]],
            axis=1,
        )
        res = jnp.dot(head_ref[...], stack, preferred_element_type=F32)
        res = jnp.maximum(res + bias_ref[...], 0.0).astype(BF16)
        out_ref[r] = res[:, 0:128]
        out_ref[r + 1] = res[:, 128:256]


def block_pair(w):
    zero = jnp.zeros_like(w)
    return jnp.concatenate(
        [jnp.concatenate([w, zero], axis=-1), jnp.concatenate([zero, w], axis=-1)], axis=-2
    )


def on_device(
    features, points_xyz, return_mask, owner_tile, bev_cell,
    meta_proj, meta_bias, conv_weight, norm_gain, head_weight, head_bias,
):
    height, breadth = return_mask.shape
    az_count = lax.axis_size("az")
    el_count = lax.axis_size("el")
    devices = az_count * el_count
    count_pts = height * breadth
    cap = 2 * count_pts // devices

    flat = jnp.concatenate(
        [
            features, points_xyz, points_xyz, points_xyz, return_mask.astype(BF16)[None],
            jnp.zeros((54, height, breadth), BF16),
        ],
        axis=0,
    )
    main = flat.transpose(1, 2, 0)

    def swap(head, tail, axis, closed):
        count = lax.axis_size(axis)
        ends = count if closed else count - 1
        return (
            lax.ppermute(tail, axis, [(i, (i + 1) % count) for i in range(ends)]),
            lax.ppermute(head, axis, [((i + 1) % count, i) for i in range(ends)]),
        )

    left, right = swap(main[:, :2], main[:, breadth - 2 :], "az", True)
    top, low = swap(
        jnp.concatenate([left[:2], main[:2], right[:2]], axis=1),
        jnp.concatenate([left[height - 2 :], main[height - 2 :], right[height - 2 :]], axis=1),
        "el",
        False,
    )

    proj = meta_proj * 0.5
    top_w = lax.reduce_precision(proj, 8, 7)
    mid_w = lax.reduce_precision(proj - top_w, 8, 7)
    low_w = lax.reduce_precision(proj - top_w - mid_w, 8, 7)
    nil = jnp.zeros((CH, CH), F32)
    tail = jnp.zeros((54, CH), F32)
    flag = jnp.ones((1, CH), F32)
    wide = []
    for l in range(2):
        wide.append(jnp.concatenate([nil, top_w[l], mid_w[l], low_w[l], 0.0 * flag, tail], axis=0))
    wide.append(jnp.concatenate([nil, jnp.zeros((9, CH), F32), flag, tail], axis=0))
    wide.append(jnp.concatenate([jnp.eye(CH, dtype=F32), jnp.zeros((10, CH), F32), tail], axis=0))
    waux = jnp.concatenate([block_pair(w) for w in wide], axis=1).astype(BF16)
    bias = jnp.concatenate([meta_bias, meta_bias], axis=1) * 0.5
    gain = jnp.concatenate([norm_gain, norm_gain], axis=1)
    conv = block_pair(conv_weight).reshape(2, 9 * 128, 128)
    mean = block_pair(jnp.full((CH, CH), 1.0 / CH, BF16))

    owners = owner_tile.reshape(-1)
    cells = bev_cell.reshape(-1)
    keep = return_mask.reshape(-1)
    ranks = slot_ranks(owners, devices)
    target = owners * cap + ranks
    member = owners[None, :] == jnp.arange(devices, dtype=jnp.int32)[:, None]
    hi = jnp.where(keep > 0, cells // 256 + 1, 0)
    lo = jnp.where(keep > 0, cells % 256 + 1, 0)
    value = jnp.stack([hi, lo], axis=0).astype(BF16)
    tile_hot = jnp.where(member[None], value[:, None, :], 0).astype(BF16)
    rank_hot = (ranks[:, None] == jnp.arange(cap, dtype=jnp.int32)[None, :]).astype(BF16)
    labels = jnp.einsum("vtp,pr->tvr", tile_hot, rank_hot, preferred_element_type=F32) - 1.0
    lanes = min(cap, 128)
    labels = labels.reshape(devices, 2, cap // lanes, lanes)
    labels = jnp.pad(
        labels, ((0, 0), (0, 0), (0, 8 - cap // lanes), (0, 128 - lanes))
    ).reshape(devices, 16, 128).astype(BF16)

    vm = pl.BlockSpec(memory_space=pltpu.VMEM)
    deep = cap // 2 + 16
    plane = pltpu.VMEM((height + 4, WIDE, 128), F32)
    msg = pl.pallas_call(
        lambda *refs: layers_kernel(height, devices, cap, *refs),
        out_shape=jax.ShapeDtypeStruct((devices, deep, 128), BF16),
        in_specs=[pl.BlockSpec(memory_space=pltpu.SMEM)] + [vm] * 11,
        out_specs=vm,
        scratch_shapes=[
            plane, plane, plane, plane,
            pltpu.VMEM((height + 2, 136, 128), F32),
            pltpu.VMEM((512, 9 * 128), BF16),
            pltpu.VMEM((count_pts, 128), F32),
            pltpu.VMEM((devices * cap, 128), F32),
            pltpu.VMEM((2, 272, 128), F32),
        ],
        compiler_params=pltpu.CompilerParams(vmem_limit_bytes=56 << 20),
        name="layers",
    )(target, main, left, right, top, low, waux, bias, gain, conv, mean, labels)

    head = head_weight.reshape(9 * CH, HEAD_CH).T
    grid = pl.pallas_call(
        lambda *refs: cells_kernel(cap, az_count, el_count, *refs),
        out_shape=jax.ShapeDtypeStruct((TILE_Y, HEAD_CH, TILE_X), BF16),
        in_specs=[vm] * 3,
        out_specs=vm,
        scratch_shapes=[
            pltpu.VMEM((devices, deep, 128), BF16),
            pltpu.VMEM((528, 256), F32),
            pltpu.VMEM((TILE_Y + 2, CH, 128), F32),
            pltpu.VMEM((4, CH, 128), BF16),
            pltpu.VMEM((8, CH, 128), BF16),
            pltpu.VMEM((6, CH, 128), F32),
            pltpu.VMEM(((TILE_Y + 2) * 3 * CH, 128), BF16),
            pltpu.SemaphoreType.DMA((devices,)),
            pltpu.SemaphoreType.DMA((devices,)),
            pltpu.SemaphoreType.DMA((8,)),
            pltpu.SemaphoreType.DMA((8,)),
        ],
        compiler_params=pltpu.CompilerParams(
            vmem_limit_bytes=56 << 20, collective_id=0, has_side_effects=True
        ),
        name="cells",
    )(msg, head, head_bias[:, None])
    return grid.transpose(1, 0, 2)


def solution(mesh):
    placed = (
        P(None, "el", "az"),
        P(None, "el", "az"),
        P("el", "az"),
        P("el", "az"),
        P("el", "az"),
        P(),
        P(),
        P(),
        P(),
        P(),
        P(),
    )
    return jax.shard_map(
        on_device, mesh=mesh, in_specs=placed, out_specs=P(None, "az", "el"), check_vma=False
    )
```

```python
import jax
import jax.numpy as jnp
from jax import lax
from jax.experimental import pallas as pl
from jax.experimental.pallas import tpu as pltpu
from jax.sharding import PartitionSpec as P

CH = 64
HEAD_CH = 128
TILE_Y = 16
TILE_X = 128
F32 = jnp.float32
BF16 = jnp.bfloat16
WIDE = 144


def slot_ranks(owners, devices):
    count_pts = owners.shape[0]
    group = min(128, count_pts)
    member = (owners[:, None] == jnp.arange(devices, dtype=jnp.int32)[None, :]).astype(BF16)
    blocks = member.reshape(count_pts // group, group, devices)
    lower = (
        lax.broadcasted_iota(jnp.int32, (group, group), 0)
        > lax.broadcasted_iota(jnp.int32, (group, group), 1)
    ).astype(BF16)
    inside = jnp.einsum("ij,bjd->bid", lower, blocks, preferred_element_type=F32)
    totals = jnp.sum(blocks, axis=1, dtype=F32)
    before = jnp.cumsum(totals, axis=0) - totals
    ranks = jnp.sum(jnp.where(blocks > 0, inside + before[:, None, :], 0.0), axis=2)
    return ranks.reshape(-1).astype(jnp.int32)


def turn_kernel(feat_ref, spot_ref, mask_ref, out_ref):
    rest = jnp.zeros((54, feat_ref.shape[2]), F32)

    @pl.loop(0, feat_ref.shape[0] // 2)
    def _(s):
        for u in range(2):
            r = s * 2 + u
            spot = spot_ref[r].astype(F32)
            flag = mask_ref[pl.ds(r, 1), :].astype(F32)
            tail = jnp.concatenate([spot, spot, spot, flag, rest], axis=0).astype(BF16)
            both = jnp.concatenate([feat_ref[r], tail], axis=0)
            out_ref[r] = jnp.transpose(both)


def layers_kernel(
    height, tiles, cap,
    tgt_ref, main_ref, left_ref, right_ref, top_ref, low_ref,
    waux_ref, bias_ref, gain_ref, conv_ref, mean_ref, lab_ref,
    msg_ref,
    q1, q2, mk, x0, x1, wt, pts, dest, line,
):
    line[...] = jnp.zeros_like(line)

    def place(slot, r):
        pair = jnp.concatenate(
            [line[slot, 0:WIDE, :].astype(BF16), line[slot, 128 : 128 + WIDE, :].astype(BF16)],
            axis=1,
        )
        got = jnp.dot(pair, waux_ref[...], preferred_element_type=F32)
        q1[r] = got[:, 0:128]
        q2[r] = got[:, 128:256]
        mk[r] = got[:, 256:384]
        x0[r] = got[:, 384:512] * (got[:, 256:384] * 0.5)

    for r in range(2):
        line[r, 0:260, :] = top_ref[r].astype(F32)
        place(r, r)
    for r in range(2):
        line[r, 0:260, :] = low_ref[r].astype(F32)
        place(r, height + 2 + r)

    @pl.loop(0, height // 2)
    def _(s):
        for u in range(2):
            r = s * 2 + u
            line[u, 0:2, :] = left_ref[r].astype(F32)
            line[u, 2:258, :] = main_ref[r].astype(F32)
            line[u, 258:260, :] = right_ref[r].astype(F32)
            place(u, r + 2)

    def layer(l, rows, width, per, q, x, qrow, qcol, emit, beside=None):
        @pl.loop(0, rows // per)
        def _(s):
            if beside is not None:
                beside(s)
            for u in range(per):
                r = s * per + u
                shift = q[r + 1 + qrow, pl.ds(1 + qcol, width), :] - bias_ref[l : l + 1, :]
                for k in range(9):
                    a, b = k // 3, k % 3
                    arg = q[r + a + qrow, pl.ds(b + qcol, width), :] - shift
                    half = x[r + a, pl.ds(b, width), :]
                    wt[pl.ds(u * width, width), k * 128 : (k + 1) * 128] = (
                        half + half * jnp.tanh(arg)
                    ).astype(BF16)
            y = jnp.dot(wt[0 : per * width, :], conv_ref[l], preferred_element_type=F32)
            ms = jnp.dot((y * y).astype(BF16), mean_ref[...], preferred_element_type=F32)
            act = jnp.maximum(y * lax.rsqrt(ms + 1e-6) * gain_ref[l : l + 1, :], 0.0)
            for u in range(per):
                r = s * per + u
                new = x[r + 1, pl.ds(1, width), :] * 2.0 + act[u * width : (u + 1) * width, :]
                new = new * mk[r + 1 + qrow, pl.ds(1 + qcol, width), :]
                emit(r, new.astype(BF16).astype(F32))

    def emit1(r, new):
        x1[r] = new * 0.5

    def emit2(r, new):
        pts[pl.ds(pl.multiple_of(r * 256, 256), 128), :] = new
        pts[pl.ds(pl.multiple_of(r * 256 + 128, 128), 128), :] = pltpu.roll(new, 64, 1)

    layer(0, height + 2, 136, 2, q1, x0, 0, 0, emit1)
    def scatter(base, count):
        for u in range(count):
            dest[pl.ds(tgt_ref[base + u], 1), :] = pts[pl.ds(base + u, 1), :]

    layer(
        1, height, 128, 4, q2, x1, 1, 1, emit2,
        lambda s: scatter(pl.multiple_of(jnp.maximum(s - 1, 0) * 1024, 1024), 1024),
    )

    @pl.loop(0, 16)
    def _(i):
        scatter((height - 4) * 256 + pl.multiple_of(i * 64, 64), 64)

    left = lax.broadcasted_iota(jnp.int32, (cap // 2, 128), 1) < 64

    @pl.loop(0, tiles)
    def _(t):
        low = dest[pl.ds(pl.multiple_of(t * cap, cap), cap // 2), :]
        high = dest[pl.ds(pl.multiple_of(t * cap + cap // 2, cap // 2), cap // 2), :]
        msg_ref[t, 0 : cap // 2, :] = jnp.where(left, low, pltpu.roll(high, 64, 1)).astype(BF16)
        msg_ref[t, cap // 2 : cap // 2 + 16, :] = lab_ref[t]


def cells_kernel(
    cap, az_count, el_count,
    msg_ref, head_ref, bias_ref,
    out_ref,
    got, acc, part, part_in, tally, tally_in, bev, edges, rims, ends, views,
    part_send, part_recv, send_sem, recv_sem, rim_send, rim_recv,
):
    az, el = lax.axis_index("az"), lax.axis_index("el")
    devices = az_count * el_count
    me = az * el_count + el
    mesh_id = pl.DeviceIdType.MESH

    barrier = pltpu.get_barrier_semaphore()

    def spot(d):
        other = lax.rem(me + d, devices)
        return other, (other // el_count, lax.rem(other, el_count))

    @pl.loop(1, devices)
    def _(d):
        pl.semaphore_signal(barrier, inc=1, device_id=spot(d)[1], device_id_type=mesh_id)

    pl.semaphore_wait(barrier, devices - 1)

    others = az_count - 1

    def message(k, d):
        column = lax.rem(el + k + 1, el_count)
        row = lax.rem(az + d, az_count)
        return pltpu.make_async_remote_copy(
            src_ref=msg_ref.at[row * el_count + column],
            dst_ref=got.at[k * others + d - 1],
            send_sem=send_sem.at[k * others + d - 1],
            recv_sem=recv_sem.at[k * others + d - 1],
            device_id=(row, el),
            device_id_type=mesh_id,
        )

    for k in range(el_count):

        @pl.loop(1, az_count)
        def _(d):
            message(k, d).start()

    half = cap // 2
    lanes = min(cap, 128)
    codes = lax.broadcasted_iota(jnp.int32, (256, 1), 0).astype(F32).astype(BF16)
    marks = lax.broadcasted_iota(jnp.int32, (16, 1), 0).astype(F32).astype(BF16)
    zero = jnp.zeros((64, cap), BF16)

    def add(block, labels):
        body = jnp.transpose(block)
        count = cap // lanes
        hi = jnp.concatenate([labels[j : j + 1, 0:lanes] for j in range(count)], axis=1)
        lo = jnp.concatenate([labels[8 + j : 9 + j, 0:lanes] for j in range(count)], axis=1)
        feat = jnp.concatenate([body[0:64, :], body[64:128, :]], axis=1)
        parts = [jnp.where(hi == jnp.array(k, BF16), feat, zero) for k in range(8)]
        parts.append(
            jnp.where(marks == hi, jnp.ones((16, cap), BF16), jnp.zeros((16, cap), BF16))
        )
        rhs = jnp.where(codes == lo, jnp.ones((256, cap), BF16), jnp.zeros((256, cap), BF16))
        return lax.dot_general(
            jnp.concatenate(parts, axis=0), rhs, (((1,), (1,)), ((), ())),
            preferred_element_type=F32,
        )

    partials = []
    for k in range(el_count):
        column = lax.rem(el + k + 1, el_count)
        own = az * el_count + column
        acc[...] = add(msg_ref[own, 0:half, :], msg_ref[own, half : half + 16, :])

        @pl.loop(1, az_count)
        def _(d):
            message(k, d).wait_recv()
            slot = k * others + d - 1
            acc[...] += add(got[slot, 0:half, :], got[slot, half : half + 16, :])

        if k < el_count - 1:
            part[k] = acc[0:512, :].astype(BF16)
            tally[k] = acc[512:528, :]
            for i, (src, dst) in enumerate(((part, part_in), (tally, tally_in))):
                copy = pltpu.make_async_remote_copy(
                    src_ref=src.at[k],
                    dst_ref=dst.at[k],
                    send_sem=part_send.at[2 * k + i],
                    recv_sem=part_recv.at[2 * k + i],
                    device_id=(az, column),
                    device_id_type=mesh_id,
                )
                copy.start()
                partials.append(copy)

    for k in range(el_count - 1):
        partials[2 * k].wait_recv()
        partials[2 * k + 1].wait_recv()
        acc[0:512, :] += part_in[k].astype(F32)
        acc[512:528, :] += tally_in[k]

    for h in range(8):
        inv = jnp.maximum(acc[512 + h : 513 + h, :], 1.0)
        mean = (acc[h * 64 : (h + 1) * 64, :] / inv).astype(BF16).astype(F32)
        bev[2 * h + 1] = mean[:, 0:128]
        bev[2 * h + 2] = mean[:, 128:256]

    lane = lax.broadcasted_iota(jnp.int32, (64, 128), 1)
    first = jnp.zeros((64, 128), F32)
    last = jnp.zeros((64, 128), F32)
    for r in range(TILE_Y):
        row = bev[r + 1]
        first = jnp.where(lane == r, row if r == 0 else pltpu.roll(row, r, 1), first)
        last = jnp.where(lane == r, pltpu.roll(row, r + 1, 1), last)
    edges[0] = first.astype(BF16)
    edges[1] = last.astype(BF16)
    edges[2] = bev[1].astype(BF16)
    edges[3] = bev[TILE_Y].astype(BF16)

    plans = []
    for dy in (-1, 0, 1):
        for dx in (-1, 0, 1):
            if dx == 0 and dy == 0:
                continue
            source = (0 if dx < 0 else 1) if dx else (2 if dy < 0 else 3)
            plans.append((dy, dx, source))
    copies = []
    for i, (dy, dx, source) in enumerate(plans):
        copy = pltpu.make_async_remote_copy(
            src_ref=edges.at[source],
            dst_ref=rims.at[i],
            send_sem=rim_send.at[i],
            recv_sem=rim_recv.at[i],
            device_id=(lax.rem(az + dy + az_count, az_count), lax.rem(el + dx + el_count, el_count)),
            device_id_type=mesh_id,
        )
        copy.start()
        copies.append(copy)

    for k in range(el_count):

        @pl.loop(1, az_count)
        def _(d):
            message(k, d).wait_send()

    for copy in partials:
        copy.wait_send()

    for copy in copies:
        copy.wait()

    def rim(y, x):
        i = [(p[0], p[1]) for p in plans].index((-y, -x))
        there = jnp.logical_and(
            jnp.logical_and(az + y >= 0, az + y < az_count),
            jnp.logical_and(el + x >= 0, el + x < el_count),
        )
        return rims[i].astype(F32) * jnp.where(there, 1.0, 0.0)

    bev[0] = rim(-1, 0)
    bev[TILE_Y + 1] = rim(1, 0)
    for j, (y, x) in enumerate([(0, -1), (0, 1), (-1, -1), (-1, 1), (1, -1), (1, 1)]):
        ends[j] = rim(y, x)
    for r in range(TILE_Y + 2):
        row = bev[r]
        if r == 0:
            lhs, rhs, at = ends[2], ends[3], TILE_Y - 1
        elif r == TILE_Y + 1:
            lhs, rhs, at = ends[4], ends[5], 0
        else:
            lhs, rhs, at = ends[0], ends[1], r - 1
        before = lhs if at == 0 else pltpu.roll(lhs, 128 - at, 1)
        after = pltpu.roll(rhs, 127 - at, 1)
        views[r * 192 : r * 192 + 64, :] = jnp.where(
            lane == 0, before, pltpu.roll(row, 1, 1)
        ).astype(BF16)
        views[r * 192 + 64 : r * 192 + 128, :] = row.astype(BF16)
        views[r * 192 + 128 : r * 192 + 192, :] = jnp.where(
            lane == 127, after, pltpu.roll(row, 127, 1)
        ).astype(BF16)

    for s in range(TILE_Y // 2):
        r = 2 * s
        stack = jnp.concatenate(
            [views[r * 192 : r * 192 + 576, :], views[(r + 1) * 192 : (r + 1) * 192 + 576, :]],
            axis=1,
        )
        res = jnp.dot(head_ref[...], stack, preferred_element_type=F32)
        res = jnp.maximum(res + bias_ref[...], 0.0).astype(BF16)
        out_ref[r] = res[:, 0:128]
        out_ref[r + 1] = res[:, 128:256]


def block_pair(w):
    zero = jnp.zeros_like(w)
    return jnp.concatenate(
        [jnp.concatenate([w, zero], axis=-1), jnp.concatenate([zero, w], axis=-1)], axis=-2
    )


def on_device(
    features, points_xyz, return_mask, owner_tile, bev_cell,
    meta_proj, meta_bias, conv_weight, norm_gain, head_weight, head_bias,
):
    height, breadth = return_mask.shape
    az_count = lax.axis_size("az")
    el_count = lax.axis_size("el")
    devices = az_count * el_count
    count_pts = height * breadth
    cap = 2 * count_pts // devices

    main = pl.pallas_call(
        turn_kernel,
        out_shape=jax.ShapeDtypeStruct((height, breadth, 128), BF16),
        in_specs=[pl.BlockSpec(memory_space=pltpu.VMEM)] * 3,
        out_specs=pl.BlockSpec(memory_space=pltpu.VMEM),
        compiler_params=pltpu.CompilerParams(vmem_limit_bytes=56 << 20),
        name="turn",
    )(features.transpose(1, 0, 2), points_xyz.transpose(1, 0, 2), return_mask)

    def swap(head, tail, axis, closed):
        count = lax.axis_size(axis)
        ends = count if closed else count - 1
        return (
            lax.ppermute(tail, axis, [(i, (i + 1) % count) for i in range(ends)]),
            lax.ppermute(head, axis, [((i + 1) % count, i) for i in range(ends)]),
        )

    left, right = swap(main[:, :2], main[:, breadth - 2 :], "az", True)
    top, low = swap(
        jnp.concatenate([left[:2], main[:2], right[:2]], axis=1),
        jnp.concatenate([left[height - 2 :], main[height - 2 :], right[height - 2 :]], axis=1),
        "el",
        False,
    )

    proj = meta_proj * 0.5
    top_w = lax.reduce_precision(proj, 8, 7)
    mid_w = lax.reduce_precision(proj - top_w, 8, 7)
    low_w = lax.reduce_precision(proj - top_w - mid_w, 8, 7)
    nil = jnp.zeros((CH, CH), F32)
    tail = jnp.zeros((54, CH), F32)
    flag = jnp.ones((1, CH), F32)
    wide = []
    for l in range(2):
        wide.append(jnp.concatenate([nil, top_w[l], mid_w[l], low_w[l], 0.0 * flag, tail], axis=0))
    wide.append(jnp.concatenate([nil, jnp.zeros((9, CH), F32), flag, tail], axis=0))
    wide.append(jnp.concatenate([jnp.eye(CH, dtype=F32), jnp.zeros((10, CH), F32), tail], axis=0))
    waux = jnp.concatenate([block_pair(w) for w in wide], axis=1).astype(BF16)
    bias = jnp.concatenate([meta_bias, meta_bias], axis=1) * 0.5
    gain = jnp.concatenate([norm_gain, norm_gain], axis=1)
    conv = block_pair(conv_weight).reshape(2, 9 * 128, 128)
    mean = block_pair(jnp.full((CH, CH), 1.0 / CH, BF16))

    owners = owner_tile.reshape(-1)
    cells = bev_cell.reshape(-1)
    keep = return_mask.reshape(-1)
    ranks = slot_ranks(owners, devices)
    target = owners * cap + ranks
    member = owners[None, :] == jnp.arange(devices, dtype=jnp.int32)[:, None]
    hi = jnp.where(keep > 0, cells // 256 + 1, 0)
    lo = jnp.where(keep > 0, cells % 256 + 1, 0)
    value = jnp.stack([hi, lo], axis=0).astype(BF16)
    tile_hot = jnp.where(member[None], value[:, None, :], 0).astype(BF16)
    rank_hot = (ranks[:, None] == jnp.arange(cap, dtype=jnp.int32)[None, :]).astype(BF16)
    labels = jnp.einsum("vtp,pr->tvr", tile_hot, rank_hot, preferred_element_type=F32) - 1.0
    lanes = min(cap, 128)
    labels = labels.reshape(devices, 2, cap // lanes, lanes)
    labels = jnp.pad(
        labels, ((0, 0), (0, 0), (0, 8 - cap // lanes), (0, 128 - lanes))
    ).reshape(devices, 16, 128).astype(BF16)

    vm = pl.BlockSpec(memory_space=pltpu.VMEM)
    deep = cap // 2 + 16
    plane = pltpu.VMEM((height + 4, WIDE, 128), F32)
    msg = pl.pallas_call(
        lambda *refs: layers_kernel(height, devices, cap, *refs),
        out_shape=jax.ShapeDtypeStruct((devices, deep, 128), BF16),
        in_specs=[pl.BlockSpec(memory_space=pltpu.SMEM)] + [vm] * 11,
        out_specs=vm,
        scratch_shapes=[
            plane, plane, plane, plane,
            pltpu.VMEM((height + 2, 136, 128), F32),
            pltpu.VMEM((512, 9 * 128), BF16),
            pltpu.VMEM((count_pts, 128), F32),
            pltpu.VMEM((devices * cap, 128), F32),
            pltpu.VMEM((2, 272, 128), F32),
        ],
        compiler_params=pltpu.CompilerParams(vmem_limit_bytes=56 << 20),
        name="layers",
    )(target, main, left, right, top, low, waux, bias, gain, conv, mean, labels)

    head = head_weight.reshape(9 * CH, HEAD_CH).T
    grid = pl.pallas_call(
        lambda *refs: cells_kernel(cap, az_count, el_count, *refs),
        out_shape=jax.ShapeDtypeStruct((TILE_Y, HEAD_CH, TILE_X), BF16),
        in_specs=[vm] * 3,
        out_specs=vm,
        scratch_shapes=[
            pltpu.VMEM((devices - el_count, deep, 128), BF16),
            pltpu.VMEM((528, 256), F32),
            pltpu.VMEM((el_count - 1, 512, 256), BF16),
            pltpu.VMEM((el_count - 1, 512, 256), BF16),
            pltpu.VMEM((el_count - 1, 16, 256), F32),
            pltpu.VMEM((el_count - 1, 16, 256), F32),
            pltpu.VMEM((TILE_Y + 2, CH, 128), F32),
            pltpu.VMEM((4, CH, 128), BF16),
            pltpu.VMEM((8, CH, 128), BF16),
            pltpu.VMEM((6, CH, 128), F32),
            pltpu.VMEM(((TILE_Y + 2) * 3 * CH, 128), BF16),
            pltpu.SemaphoreType.DMA((2 * el_count - 2,)),
            pltpu.SemaphoreType.DMA((2 * el_count - 2,)),
            pltpu.SemaphoreType.DMA((devices - el_count,)),
            pltpu.SemaphoreType.DMA((devices - el_count,)),
            pltpu.SemaphoreType.DMA((8,)),
            pltpu.SemaphoreType.DMA((8,)),
        ],
        compiler_params=pltpu.CompilerParams(
            vmem_limit_bytes=56 << 20, collective_id=0, has_side_effects=True
        ),
        name="cells",
    )(msg, head, head_bias[:, None])
    return grid.transpose(1, 0, 2)


def solution(mesh):
    placed = (
        P(None, "el", "az"),
        P(None, "el", "az"),
        P("el", "az"),
        P("el", "az"),
        P("el", "az"),
        P(),
        P(),
        P(),
        P(),
        P(),
        P(),
    )
    return jax.shard_map(
        on_device, mesh=mesh, in_specs=placed, out_specs=P(None, "az", "el"), check_vma=False
    )
```
